256 devices in a mesh: row: 16 (over z_hi, x, core), col: 16 (over z_lo, y).
Axes of the slice: x: 4, y: 4, z: 8 (z_hi: 2, z_lo: 4; z = z_hi * 4 + z_lo), core: 2. Of those that a mesh axis runs over, the one named last changes fastest.
Arguments:
- inputs: bfloat16 [2048, 6144], P('col', 'row'), may hold values from -6 to 6
- w_in: bfloat16 [6144, 24576], P('row', 'col'), may hold values from -0.078125 to 0.078125
- b_in: bfloat16 [24576], P('col'), may hold values from -4 to 4
- w_out: bfloat16 [24576, 6144], P('col', 'row'), may hold values from -0.0390625 to 0.0390625
- b_out: bfloat16 [6144], P('row'), may hold values from -4 to 4
- grad_out: bfloat16 [2048, 6144], P('col', 'row'), may hold values from -3 to 3
Outputs:
- block_out: bfloat16 [2048, 6144], P('col', 'row')
- grad_inputs: bfloat16 [2048, 6144], P('col', 'row')
- grad_w_in: float32 [6144, 24576], P('row', 'col')
- grad_w_out: float32 [24576, 6144], P('col', 'row')
- grad_b_in: float32 [24576], P('col')
- grad_b_out: float32 [6144], P('row')
The draws below stay inside these ranges and needn't reach their ends.
All inputs are finite; a program needn't handle non-finite values.
Results may differ from the reference program's by a relative error of at most 0.03.
Values may be sent and summed in bfloat16 or wider, within the bound.
No kernel may reach another device: no remote copies, remote signals or barrier semaphores. Data moves between devices by JAX's collectives and lax.ppermute only.
A program may use at most 128 MiB of HBM per device.

```python
import jax
import jax.numpy as jnp
from jax import lax

D = 6144
FF = 24576
TOKENS = 2048
N_ROW = 16
N_COL = 16


def levels(key, extent, shards, least, largest):
    level = 1.0
    for dim, parts in shards:
        steps = jax.random.uniform(jax.random.fold_in(jax.random.fold_in(key, 6), dim), (parts,), jnp.float32, least / len(shards), largest / len(shards))
        level = level * jnp.repeat(jnp.exp(steps), extent[dim] // parts).reshape((-1,) + (1,) * (len(extent) - 1 - dim))
    return level


def normal_values(rng, dims, spread, reach, shards=(), held_as=jnp.bfloat16):
    gain = levels(rng, dims, shards, -0.22, 0.18) if shards else 1.0
    drawn = jax.random.normal(rng, dims, jnp.float32) * spread * gain
    return jnp.minimum(jnp.maximum(drawn, -reach), reach).astype(held_as)


def setup_inputs(seed: int = 0) -> dict:
    seeds = jax.random.split(jax.random.key(seed), 7)
    inputs = normal_values(seeds[0], (TOKENS, D), 1.0, 6.0, ((0, 16), (1, 16)))
    w_in = normal_values(seeds[1], (D, FF), D ** -0.5, 0.078125, ((0, 16), (1, 16)))
    b_in = normal_values(seeds[2], (FF,), 1.0, 4.0, ((0, 16),))
    w_out = normal_values(seeds[3], (FF, D), FF ** -0.5, 0.0390625, ((0, 16), (1, 16)))
    b_out = normal_values(seeds[4], (D,), 1.0, 4.0, ((0, 16),))
    grad_out = normal_values(seeds[5], (TOKENS, D), 0.5, 3.0, ((0, 16), (1, 16)))
    return dict(inputs=inputs, w_in=w_in, b_in=b_in, w_out=w_out, b_out=b_out, grad_out=grad_out)


def rounded(matrix):
    lowered = lax.optimization_barrier(matrix.astype(jnp.bfloat16))
    return lowered.astype(jnp.float32)

def blocked_product(left, right, blocks):
    width_block = left.shape[1] // blocks

    def add_block(total, block_index):
        offset = block_index * width_block
        left_piece = lax.dynamic_slice_in_dim(left, offset, width_block, 1)
        right_piece = lax.dynamic_slice_in_dim(right, offset, width_block, 0)
        partial_sum = jnp.dot(left_piece, right_piece, preferred_element_type=jnp.float32)
        return (total + rounded(partial_sum), None)
    zeros_sum = jnp.zeros((left.shape[0], right.shape[1]), jnp.float32)
    return lax.scan(add_block, zeros_sum, jnp.arange(blocks, dtype=jnp.int32))[0]

def activate(preact):
    return jax.nn.gelu(preact, approximate=True)

def reference(inputs, w_in, b_in, w_out, b_out, grad_out):
    preact = blocked_product(inputs, w_in, N_ROW) + b_in.astype(jnp.float32)
    hidden, pullback = jax.vjp(activate, preact)
    hidden = hidden.astype(jnp.bfloat16)
    block_out = (blocked_product(hidden, w_out, N_COL) + b_out.astype(jnp.float32)).astype(jnp.bfloat16)
    grad_hidden = blocked_product(grad_out, w_out.T, N_ROW)
    grad_pre = pullback(grad_hidden)[0].astype(jnp.bfloat16)
    grad_w_out = jnp.dot(hidden.T, grad_out, preferred_element_type=jnp.float32)
    grad_w_in = jnp.dot(inputs.T, grad_pre, preferred_element_type=jnp.float32)
    grad_b_in = lax.optimization_barrier(jnp.sum(grad_pre.astype(jnp.float32), axis=0))
    grad_b_out = lax.optimization_barrier(jnp.sum(grad_out.astype(jnp.float32), axis=0))
    grad_inputs = blocked_product(grad_pre, w_in.T, N_COL).astype(jnp.bfloat16)
    return (block_out, grad_inputs, grad_w_in, grad_w_out, grad_b_in, grad_b_out)
```

```python
import jax
import jax.numpy as jnp
from jax import lax
from jax.sharding import PartitionSpec as P

BF = jnp.bfloat16
F32 = jnp.float32


def row_swap(value, mask):
    return lax.ppermute(value, "row", [(i, i ^ mask) for i in range(16)])


def col_swap(value, mask):
    return lax.ppermute(value, "col", [(i, i ^ mask) for i in range(16)])


def core_swap(value):
    return row_swap(value, 1)


def x_swap(value, r):
    return row_swap(value, r << 1)


def zh_swap(value):
    return row_swap(value, 8)


def y_swap(value, r):
    return col_swap(value, r)


def zl_swap(value, r):
    return col_swap(value, r << 2)


def ring_gather(value, swap):
    half = value.shape[0] // 2
    from1, from3 = swap(value, 1), swap(value, 3)
    from2 = jnp.concatenate([swap(from1[:half], 3), swap(from3[half:], 1)], axis=0)
    return [value, from1, from2, from3]


def ring_scatter(part, swap):
    across = part(2).astype(BF)
    half = across.shape[0] // 2
    for1, for3 = swap(across[:half], 1), swap(across[half:], 3)
    to3 = part(3)
    to3 = jnp.concatenate([to3[:half] + for1.astype(F32), to3[half:]], axis=0).astype(BF)
    to1 = part(1)
    to1 = jnp.concatenate([to1[:half], to1[half:] + for3.astype(F32)], axis=0).astype(BF)
    got1, got3 = swap(to1, 1), swap(to3, 3)
    return part(0) + got1.astype(F32) + got3.astype(F32)


def activate(preact):
    return jax.nn.gelu(preact, approximate=True)


def mm(a, b):
    return jnp.dot(a, b, preferred_element_type=F32)


def per_device(inputs, w_in, b_in, w_out, b_out, grad_out):
    row = lax.axis_index("row")
    core = row & 1
    x = (row >> 1) & 3
    tokens, feats = inputs.shape
    mine = tokens // 2
    hid = w_in.shape[1]

    def own_tokens(value):
        keep = lax.dynamic_slice_in_dim(value, core * mine, mine, 0)
        give = lax.dynamic_slice_in_dim(value, (1 - core) * mine, mine, 0)
        return jnp.concatenate([keep, core_swap(give)], axis=1)

    def gather_tokens(value):
        block = own_tokens(value)
        blocks = jnp.stack([block] + [zl_swap(block, r) for r in (1, 2, 3)])
        whole = jnp.stack(ring_gather(blocks, y_swap), axis=1)
        return [
            lax.dynamic_index_in_dim(whole, x ^ r, 0, keepdims=False).reshape(4 * mine, 2 * feats)
            for r in range(4)
        ]

    xs = gather_tokens(inputs)
    win = jnp.concatenate([w_in, core_swap(w_in)], axis=0)
    wout = jnp.concatenate([w_out, core_swap(w_out)], axis=1)
    gs = gather_tokens(grad_out)

    pre = ring_scatter(lambda r: mm(xs[r], win), x_swap).astype(BF)
    pre = pre.astype(F32) + zh_swap(pre).astype(F32) + b_in.astype(F32)
    hidden, pullback = jax.vjp(activate, pre)
    hs = ring_gather(hidden.astype(BF), x_swap)

    gh = ring_scatter(
        lambda r: jnp.einsum("td,fd->tf", gs[r], wout, preferred_element_type=F32), x_swap
    ).astype(BF)
    gh = gh.astype(F32) + zh_swap(gh).astype(F32)
    grad_pre = pullback(gh)[0].astype(BF)
    ps = ring_gather(grad_pre, x_swap)

    def scatter_tokens(blocks, weight, spec):
        whole = jnp.stack([
            jnp.einsum(spec, b, weight, preferred_element_type=F32).reshape(4, mine, 2 * feats)
            for b in blocks
        ])
        summed = ring_scatter(lambda r: whole[:, r], y_swap)
        total = lax.dynamic_index_in_dim(summed, x, 0, keepdims=False)
        sent = summed.astype(BF)
        for r in (1, 2, 3):
            total = total + zl_swap(
                lax.dynamic_index_in_dim(sent, x ^ r, 0, keepdims=False), r
            ).astype(F32)
        return total

    def all_tokens(total):
        keep, got = total[:, :feats], core_swap(total[:, feats:])
        return jnp.where(
            core == 0,
            jnp.concatenate([keep, got], axis=0),
            jnp.concatenate([got, keep], axis=0),
        )

    block_out = all_tokens(scatter_tokens(hs, wout, "tf,fd->td"))
    block_out = (block_out + b_out.astype(F32)).astype(BF)
    grad_inputs = all_tokens(scatter_tokens(ps, win, "tf,df->td").astype(BF))

    h_all = jnp.concatenate(hs, axis=0)
    p_all = jnp.concatenate(ps, axis=0)
    x_all = jnp.concatenate(xs, axis=0)
    g_all = jnp.concatenate(gs, axis=0)

    gw_out = jnp.einsum("tf,td->fd", h_all, g_all, preferred_element_type=F32)
    grad_w_out = gw_out[:, :feats] + core_swap(gw_out[:, feats:].astype(BF)).astype(F32)
    gw_in = jnp.einsum("td,tf->df", x_all, p_all, preferred_element_type=F32)
    grad_w_in = gw_in[:feats] + core_swap(gw_in[feats:].astype(BF)).astype(F32)
    gb_in = jnp.sum(p_all, axis=0, dtype=F32)
    grad_b_in = gb_in + core_swap(gb_in)
    gb_out = jnp.sum(g_all, axis=0, dtype=F32)
    grad_b_out = gb_out[:feats] + core_swap(gb_out[feats:])
    return (block_out, grad_inputs, grad_w_in, grad_w_out, grad_b_in, grad_b_out)


def solution(mesh):
    in_specs = (
        P("col", "row"),
        P("row", "col"),
        P("col"),
        P("col", "row"),
        P("row"),
        P("col", "row"),
    )
    out_specs = (
        P("col", "row"),
        P("col", "row"),
        P("row", "col"),
        P("col", "row"),
        P("col"),
        P("row"),
    )
    return jax.shard_map(
        per_device, mesh=mesh, in_specs=in_specs, out_specs=out_specs, check_vma=False
    )
```

```python
import jax
import jax.numpy as jnp
from jax import lax
from jax.sharding import PartitionSpec as P

BF = jnp.bfloat16
F32 = jnp.float32


def row_swap(value, mask):
    return lax.ppermute(value, "row", [(i, i ^ mask) for i in range(16)])


def col_swap(value, mask):
    return lax.ppermute(value, "col", [(i, i ^ mask) for i in range(16)])


def core_swap(value):
    return row_swap(value, 1)


def x_swap(value, r):
    return row_swap(value, r << 1)


def zh_swap(value):
    return row_swap(value, 8)


def y_swap(value, r):
    return col_swap(value, r)


def zl_swap(value, r):
    return col_swap(value, r << 2)


def after(value, gate):
    return lax.optimization_barrier((value, gate))[0]


def phase(gate, *sends):
    values = lax.optimization_barrier(([v for _, _, v in sends], gate))[0]
    return [swap(v) if r is None else swap(v, r) for (swap, r, _), v in zip(sends, values)]


def activate(preact):
    return jax.nn.gelu(preact, approximate=True)


def mm(a, b):
    return jnp.dot(a, b, preferred_element_type=F32)


def mm_t(a, b):
    return jnp.einsum("tk,nk->tn", a, b, preferred_element_type=F32)


def per_device(inputs, w_in, b_in, w_out, b_out, grad_out):
    row = lax.axis_index("row")
    core = row & 1
    x = (row >> 1) & 3
    tokens, feats = inputs.shape
    mine = tokens // 2
    two = 2 * mine

    def own_tokens(value):
        keep = lax.dynamic_slice_in_dim(value, core * mine, mine, 0)
        give = lax.dynamic_slice_in_dim(value, (1 - core) * mine, mine, 0)
        return lambda gate: jnp.concatenate([keep, phase(gate, (core_swap, None, give))[0]], axis=1)

    def quarters(ys):
        return [
            jnp.concatenate(
                [lax.dynamic_index_in_dim(y, x ^ r, 0, keepdims=False) for y in ys], axis=0
            )
            for r in range(4)
        ]

    def cat(*pieces):
        return jnp.concatenate(pieces, axis=0)

    def padded(value, before, behind):
        return lax.pad(
            value, jnp.zeros((), BF), ((before, behind, 0), (0, 0, 0))
        ).astype(F32)

    def near(part1, part3, got1, got3):
        n = got1.shape[0]
        return (part1 + padded(got3, n, 0)).astype(BF), (part3 + padded(got1, 0, n)).astype(BF)

    def total(part, got1, got3):
        return (part + got1.astype(F32) + got3.astype(F32)).astype(BF)

    def zl_sends(block):
        return tuple((zl_swap, r, block) for r in (1, 2, 3))

    f_block = own_tokens(inputs)(())
    b_block = own_tokens(grad_out)(())
    *g1, w_in_got = phase(f_block, *zl_sends(f_block), (core_swap, None, w_in))
    g2 = phase(f_block, *zl_sends(b_block))
    f0 = jnp.stack([f_block] + g1)
    win = cat(w_in, w_in_got)
    f1, f3 = phase((g1, win), (y_swap, 1, f0), (y_swap, 3, f0))
    b0 = jnp.stack([b_block] + g2)
    xs0 = quarters([f0, f1])

    p0 = [mm(t, win) for t in xs0]
    far0 = p0[2].astype(BF)
    far01, far03, got1, got3, w_out_got = phase(
        (f1, f3, g2),
        (x_swap, 1, far0[:mine]),
        (x_swap, 3, far0[mine:]),
        (y_swap, 1, cat(f3[2:], b0[:2])),
        (y_swap, 3, cat(f1[:2], b0[2:])),
        (core_swap, None, w_out),
    )
    wout = jnp.concatenate([w_out, w_out_got], axis=1)
    f2 = cat(got3[:2], got1[:2])
    b1a, b3b = got1[2:], got3[2:]
    xs1 = quarters([f2, f3])

    p1 = [mm(t, win) for t in xs1]
    far1 = p1[2].astype(BF)
    to1, to3 = near(p0[1], p0[3], far01, far03)
    got1, got3, y1, y3 = phase(
        (far01, far03, got1, got3, w_out_got),
        (x_swap, 1, cat(to1, far1[:mine])),
        (x_swap, 3, cat(to3, far1[mine:])),
        (y_swap, 1, cat(b0[2:], b3b)),
        (y_swap, 3, cat(b0[:2], b1a)),
    )
    pre0 = total(p0[0], got1[:two], got3[:two])
    far11, far13 = got1[two:], got3[two:]
    gs = quarters([b0, cat(b1a, y1[:2]), cat(y3[2:], y1[2:]), cat(y3[:2], b3b)])

    q = [mm_t(t, wout) for t in gs]
    qfar = q[2].astype(BF)
    to1, to3 = near(p1[1], p1[3], far11, far13)
    to1, to3 = cat(to1, qfar[:two]), cat(to3, qfar[two:])
    z0, got1, got3 = phase(
        (got1, got3, y1, y3, to1, to3),
        (zh_swap, None, pre0),
        (x_swap, 1, to1),
        (x_swap, 3, to3),
    )
    pre1 = total(p1[0], got1[:two], got3[:two])

    to1, to3 = near(q[1], q[3], got1[two:], got3[two:])
    z1, got1, got3 = phase(
        (z0, got1, got3, to1, to3), (zh_swap, None, pre1), (x_swap, 1, to1), (x_swap, 3, to3)
    )
    gh = total(q[0], got1, got3)

    def preact(part, z):
        return part.astype(F32) + z.astype(F32) + b_in.astype(F32)

    def grad_of(part, z, pre, pre_z):
        part, z, pre, pre_z = lax.optimization_barrier((part, z, pre, pre_z))
        pull = jax.vjp(activate, preact(pre, pre_z))[1]
        return pull(part.astype(F32) + z.astype(F32))[0].astype(BF)

    h0 = after(activate(preact(pre0, z0)).astype(BF), (to1, to3))
    h = cat(h0, after(activate(preact(pre1, z1)).astype(BF), ()))
    zq1, h1, h3 = phase(
        (z1, got1, got3, h), (zh_swap, None, gh[two:]), (x_swap, 1, h), (x_swap, 3, h)
    )

    d1 = grad_of(gh[two:], zq1, pre1, z1)
    to1, to3 = cat(d1, h3[two:]), cat(d1, h1[:two])
    zq0, got1, got3 = phase(
        (zq1, h1, h3, to1, to3), (zh_swap, None, gh[:two]), (x_swap, 1, to1), (x_swap, 3, to3)
    )
    hs = [h, h1, cat(got3[two:], got1[two:]), h3]
    d11, d13 = got1[:two], got3[:two]

    def y_parts(blocks, weight, product):
        outs = [product(b, weight) for b in blocks]
        outs = [o.reshape(-1, mine, 2 * feats) for o in outs]
        return [[o[k] for o in outs] for k in range(outs[0].shape[0])]

    def y_far_sends(part):
        return (y_swap, 1, jnp.stack(part[:2]).astype(BF)), (y_swap, 3, jnp.stack(part[2:]).astype(BF))

    def y_near_sends(part1, part3, got1, got3):
        to3 = jnp.stack([part3[0] + got1[0], part3[1] + got1[1], part3[2], part3[3]]).astype(BF)
        to1 = jnp.stack([part1[0], part1[1], part1[2] + got3[0], part1[3] + got3[1]]).astype(BF)
        return (y_swap, 1, to1), (y_swap, 3, to3)

    def zl_split(part0, got1, got3):
        summed = jnp.stack(part0) + got1.astype(F32) + got3.astype(F32)
        sent = summed.astype(BF)
        pick = lambda a, r: lax.dynamic_index_in_dim(a, x ^ r, 0, keepdims=False)
        return pick(summed, 0), tuple((zl_swap, r, pick(sent, r)) for r in (1, 2, 3))

    def zl_total(own, got):
        return own + sum(g.astype(F32) for g in got)

    def all_tokens(keep, got):
        return jnp.where(core == 0, cat(keep, got), cat(got, keep))

    d0 = grad_of(gh[:two], zq0, pre0, z0)
    p6 = (zq0, got1, got3)
    to1, to3 = cat(d0, d13[mine:]), cat(d0, d11[:mine])
    g_all = cat(*gs)
    gb_out = jnp.sum(after(g_all, zq1), axis=0, dtype=F32)
    got1, got3, gb_out_got = phase(
        p6, (x_swap, 1, to1), (x_swap, 3, to3), (core_swap, None, after(gb_out[feats:], (to1, to3)))
    )
    o0, o1, o2, o3 = y_parts(hs, wout, mm)
    ofar = phase((p6, gb_out_got), *y_far_sends(o2))
    h_all, g_late = after((cat(*hs), g_all), ofar)
    gw_out = jnp.einsum("tf,td->fd", h_all, g_late, preferred_element_type=F32)
    ps1 = [d1, d11, cat(got3[two:], got1[two:]), d13]
    d01, d03 = got1[:two], got3[:two]

    i2, i3 = y_parts(ps1, win, mm_t)
    p7 = (got1, got3, ofar, gw_out)
    to1, to3 = (
        cat(far[2], own[2]) for far, own in zip(y_far_sends(i2), y_near_sends(o1, o3, *ofar))
    )
    relayed0, relayed1, got1, got3, gw_out_got = phase(
        p7,
        (x_swap, 3, d01[:mine]),
        (x_swap, 1, d03[mine:]),
        (y_swap, 1, to1),
        (y_swap, 3, to3),
        (core_swap, None, gw_out[:, feats:].astype(BF)),
    )
    ifar, onear = (got1[:2], got3[:2]), (got1[2:], got3[2:])
    ps0 = [d0, d01, cat(relayed0, relayed1), d03]

    i0, i1 = y_parts(ps0, win, mm_t)
    o_own, o_sends = zl_split(o0, *onear)
    i_sends = y_near_sends(i1, i3, *ifar)
    inear0, inear1, *o_got = phase((relayed0, relayed1, got1, got3, gw_out_got), *i_sends, *o_sends)
    inear = (inear0, inear1)
    x_all, p_all = after((cat(*xs0, *xs1), cat(*ps0, *ps1)), [v for _, _, v in i_sends])
    gw_in = jnp.einsum("td,tf->df", x_all, p_all, preferred_element_type=F32)
    gb_in = jnp.sum(p_all, axis=0, dtype=F32)
    grad_w_out = gw_out[:, :feats] + gw_out_got.astype(F32)
    grad_b_out = gb_out[:feats] + gb_out_got

    i_own, i_sends = zl_split(i0, *inear)
    o_total = zl_total(o_own, o_got)
    *i_got, o_other, gw_in_got = phase(
        (inear, o_got, grad_w_out),
        *i_sends,
        (core_swap, None, o_total[:, feats:]),
        (core_swap, None, gw_in[feats:].astype(BF)),
    )
    block_out = (all_tokens(o_total[:, :feats], o_other) + b_out.astype(F32)).astype(BF)
    grad_w_in = gw_in[:feats] + gw_in_got.astype(F32)
    i_total = zl_total(i_own, i_got).astype(BF)

    i_other, gb_in_got = phase(
        (block_out, i_got), (core_swap, None, i_total[:, feats:]), (core_swap, None, gb_in)
    )
    grad_b_in = gb_in + gb_in_got
    grad_inputs = all_tokens(i_total[:, :feats], i_other)
    return (block_out, grad_inputs, grad_w_in, grad_w_out, grad_b_in, grad_b_out)


def solution(mesh):
    in_specs = (
        P("col", "row"),
        P("row", "col"),
        P("col"),
        P("col", "row"),
        P("row"),
        P("col", "row"),
    )
    out_specs = (
        P("col", "row"),
        P("col", "row"),
        P("row", "col"),
        P("col", "row"),
        P("col"),
        P("row"),
    )
    return jax.shard_map(
        per_device, mesh=mesh, in_specs=in_specs, out_specs=out_specs, check_vma=False
    )
```

```python
import jax
import jax.numpy as jnp
from jax import lax
from jax.sharding import PartitionSpec as P

BF = jnp.bfloat16
F32 = jnp.float32


def row_swap(value, mask):
    return lax.ppermute(value, "row", [(i, i ^ mask) for i in range(16)])


def col_swap(value, mask):
    return lax.ppermute(value, "col", [(i, i ^ mask) for i in range(16)])


def core_swap(value):
    return row_swap(value, 1)


def x_swap(value, r):
    return row_swap(value, r << 1)


def zh_swap(value):
    return row_swap(value, 8)


def y_swap(value, r):
    return col_swap(value, r)


def zl_swap(value, r):
    return col_swap(value, r << 2)


def after(value, gate):
    return lax.optimization_barrier((value, gate))[0]


def phase(gate, *sends):
    values = lax.optimization_barrier(([v for _, _, v in sends], gate))[0]
    return [swap(v) if r is None else swap(v, r) for (swap, r, _), v in zip(sends, values)]


def activate(preact):
    return jax.nn.gelu(preact, approximate=True)


def mm(a, b):
    return jnp.dot(a, b, preferred_element_type=F32)


def mm_t(a, b):
    return jnp.einsum("tk,nk->tn", a, b, preferred_element_type=F32)


def per_device(inputs, w_in, b_in, w_out, b_out, grad_out):
    row = lax.axis_index("row")
    core = row & 1
    x = (row >> 1) & 3
    tokens, feats = inputs.shape
    mine = tokens // 2
    two = 2 * mine

    def own_tokens(value):
        keep = lax.dynamic_slice_in_dim(value, core * mine, mine, 0)
        give = lax.dynamic_slice_in_dim(value, (1 - core) * mine, mine, 0)
        return lambda gate: jnp.concatenate([keep, phase(gate, (core_swap, None, give))[0]], axis=1)

    def quarters(ys):
        return [
            jnp.concatenate(
                [lax.dynamic_index_in_dim(y, x ^ r, 0, keepdims=False) for y in ys], axis=0
            )
            for r in range(4)
        ]

    def cat(*pieces):
        return jnp.concatenate(pieces, axis=0)

    def padded(value, before, behind):
        return lax.pad(
            value, jnp.zeros((), BF), ((before, behind, 0), (0, 0, 0))
        ).astype(F32)

    def near(part1, part3, got1, got3):
        n = got1.shape[0]
        return (part1 + padded(got3, n, 0)).astype(BF), (part3 + padded(got1, 0, n)).astype(BF)

    def total(part, got1, got3):
        return (part + got1.astype(F32) + got3.astype(F32)).astype(BF)

    def zl_sends(block):
        return tuple((zl_swap, r, block) for r in (1, 2, 3))

    f_block = own_tokens(inputs)(())
    *g1, w_in_got = phase(f_block, *zl_sends(f_block), (core_swap, None, w_in))
    f0 = jnp.stack([f_block] + g1)
    win = cat(w_in, w_in_got)
    f1, f3 = phase((g1, win), (y_swap, 1, f0), (y_swap, 3, f0))
    b_block = own_tokens(grad_out)((g1, win))
    g2 = phase(g1, *zl_sends(b_block))
    b0 = jnp.stack([b_block] + g2)
    xs0 = quarters([f0, f1])

    p0 = [mm(t, win) for t in xs0]
    far0 = p0[2].astype(BF)
    far01, far03, got1, got3, w_out_got = phase(
        (f1, f3, g2),
        (x_swap, 1, far0[:mine]),
        (x_swap, 3, far0[mine:]),
        (y_swap, 1, cat(f3[2:], b0[:2])),
        (y_swap, 3, cat(f1[:2], b0[2:])),
        (core_swap, None, w_out),
    )
    wout = jnp.concatenate([w_out, w_out_got], axis=1)
    f2 = cat(got3[:2], got1[:2])
    b1a, b3b = got1[2:], got3[2:]
    xs1 = quarters([f2, f3])

    p1 = [mm(t, win) for t in xs1]
    far1 = p1[2].astype(BF)
    to1, to3 = near(p0[1], p0[3], far01, far03)
    got1, got3, y1, y3 = phase(
        (far01, far03, got1, got3, w_out_got),
        (x_swap, 1, cat(to1, far1[:mine])),
        (x_swap, 3, cat(to3, far1[mine:])),
        (y_swap, 1, cat(b0[2:], b3b)),
        (y_swap, 3, cat(b0[:2], b1a)),
    )
    pre0 = total(p0[0], got1[:two], got3[:two])
    far11, far13 = got1[two:], got3[two:]
    gs = quarters([b0, cat(b1a, y1[:2]), cat(y3[2:], y1[2:]), cat(y3[:2], b3b)])

    q = [mm_t(t, wout) for t in gs]
    qfar = q[2].astype(BF)
    to1, to3 = near(p1[1], p1[3], far11, far13)
    to1, to3 = cat(to1, qfar[:two]), cat(to3, qfar[two:])
    z0, got1, got3 = phase(
        (got1, got3, y1, y3, to1, to3),
        (zh_swap, None, pre0),
        (x_swap, 1, to1),
        (x_swap, 3, to3),
    )
    pre1 = total(p1[0], got1[:two], got3[:two])

    to1, to3 = near(q[1], q[3], got1[two:], got3[two:])
    z1, got1, got3 = phase(
        (z0, got1, got3, to1, to3), (zh_swap, None, pre1), (x_swap, 1, to1), (x_swap, 3, to3)
    )
    gh = total(q[0], got1, got3)

    def preact(part, z):
        return part.astype(F32) + z.astype(F32) + b_in.astype(F32)

    def grad_of(part, z, pre, pre_z):
        part, z, pre, pre_z = lax.optimization_barrier((part, z, pre, pre_z))
        pull = jax.vjp(activate, preact(pre, pre_z))[1]
        return pull(part.astype(F32) + z.astype(F32))[0].astype(BF)

    h0 = after(activate(preact(pre0, z0)).astype(BF), (to1, to3))
    h = cat(h0, after(activate(preact(pre1, z1)).astype(BF), ()))
    zq1, h1, h3 = phase(
        (z1, got1, got3, h), (zh_swap, None, gh[two:]), (x_swap, 1, h), (x_swap, 3, h)
    )

    d1 = grad_of(gh[two:], zq1, pre1, z1)
    to1, to3 = cat(d1, h3[two:]), cat(d1, h1[:two])
    zq0, got1, got3 = phase(
        (zq1, h1, h3, to1, to3), (zh_swap, None, gh[:two]), (x_swap, 1, to1), (x_swap, 3, to3)
    )
    hs = [h, h1, cat(got3[two:], got1[two:]), h3]
    d11, d13 = got1[:two], got3[:two]

    def y_parts(blocks, weight, product):
        outs = [product(b, weight) for b in blocks]
        outs = [o.reshape(-1, mine, 2 * feats) for o in outs]
        return [[o[k] for o in outs] for k in range(outs[0].shape[0])]

    def y_far_sends(part):
        return (y_swap, 1, jnp.stack(part[:2]).astype(BF)), (y_swap, 3, jnp.stack(part[2:]).astype(BF))

    def y_near_sends(part1, part3, got1, got3):
        to3 = jnp.stack([part3[0] + got1[0], part3[1] + got1[1], part3[2], part3[3]]).astype(BF)
        to1 = jnp.stack([part1[0], part1[1], part1[2] + got3[0], part1[3] + got3[1]]).astype(BF)
        return (y_swap, 1, to1), (y_swap, 3, to3)

    def zl_split(part0, got1, got3):
        summed = jnp.stack(part0) + got1.astype(F32) + got3.astype(F32)
        sent = summed.astype(BF)
        pick = lambda a, r: lax.dynamic_index_in_dim(a, x ^ r, 0, keepdims=False)
        return pick(summed, 0), tuple((zl_swap, r, pick(sent, r)) for r in (1, 2, 3))

    def zl_total(own, got):
        return own + sum(g.astype(F32) for g in got)

    def all_tokens(keep, got):
        return jnp.where(core == 0, cat(keep, got), cat(got, keep))

    d0 = grad_of(gh[:two], zq0, pre0, z0)
    p6 = (zq0, got1, got3)
    to1, to3 = cat(d0, d13[mine:]), cat(d0, d11[:mine])
    g_all = cat(*gs)
    gb_out = jnp.sum(after(g_all, zq1), axis=0, dtype=F32)
    got1, got3, gb_out_got = phase(
        p6, (x_swap, 1, to1), (x_swap, 3, to3), (core_swap, None, after(gb_out[feats:], (to1, to3)))
    )
    o0, o1, o2, o3 = y_parts(hs, wout, mm)
    ofar = phase((p6, gb_out_got), *y_far_sends(o2))
    onear = phase(ofar, *y_near_sends(o1, o3, *ofar))
    h_all, g_late = after((cat(*hs), g_all), (got1, got3, ofar))
    gw_out = jnp.einsum("tf,td->fd", h_all, g_late, preferred_element_type=F32)
    ps1 = [d1, d11, cat(got3[two:], got1[two:]), d13]
    d01, d03 = got1[:two], got3[:two]

    i2, i3 = y_parts(ps1, win, mm_t)
    relayed0, relayed1, *ifar = phase(
        (got1, got3, ofar),
        (x_swap, 3, d01[:mine]),
        (x_swap, 1, d03[mine:]),
        *y_far_sends(i2),
    )
    (gw_out_got,) = phase((got1, got3), (core_swap, None, gw_out[:, feats:].astype(BF)))
    ps0 = [d0, d01, cat(relayed0, relayed1), d03]

    i0, i1 = y_parts(ps0, win, mm_t)
    o_own, o_sends = zl_split(o0, *onear)
    i_sends = y_near_sends(i1, i3, *ifar)
    p8 = (relayed0, relayed1, ifar, onear, gw_out_got)
    near_ready = [v for _, _, v in i_sends]
    inear = phase(p8, *i_sends)
    gb_in = jnp.sum(cat(*ps0, *ps1), axis=0, dtype=F32)
    (gb_in_got,) = phase((p8, near_ready), (core_swap, None, gb_in))
    o_got = phase(gb_in_got, *o_sends)
    x_all, p_all = after((cat(*xs0, *xs1), cat(*ps0, *ps1)), gb_in_got)
    gw_in = jnp.einsum("td,tf->df", x_all, p_all, preferred_element_type=F32)
    grad_b_in = gb_in + gb_in_got
    grad_w_out = gw_out[:, :feats] + gw_out_got.astype(F32)
    grad_b_out = gb_out[:feats] + gb_out_got

    i_own, i_sends = zl_split(i0, *inear)
    o_total = zl_total(o_own, o_got)
    *i_got, gw_in_got = phase(inear, *i_sends, (core_swap, None, gw_in[feats:].astype(BF)))
    grad_w_in = gw_in[:feats] + gw_in_got.astype(F32)
    i_total = zl_total(i_own, i_got).astype(BF)

    i_other, o_other = phase(
        (i_got, o_got, grad_w_in, grad_w_out, grad_b_in, grad_b_out),
        (core_swap, None, i_total[:, feats:]),
        (core_swap, None, o_total[:, feats:]),
    )
    block_out = (all_tokens(o_total[:, :feats], o_other) + b_out.astype(F32)).astype(BF)
    grad_inputs = all_tokens(i_total[:, :feats], i_other)
    return (block_out, grad_inputs, grad_w_in, grad_w_out, grad_b_in, grad_b_out)


def solution(mesh):
    in_specs = (
        P("col", "row"),
        P("row", "col"),
        P("col"),
        P("col", "row"),
        P("row"),
        P("col", "row"),
    )
    out_specs = (
        P("col", "row"),
        P("col", "row"),
        P("row", "col"),
        P("col", "row"),
        P("col"),
        P("row"),
    )
    return jax.shard_map(
        per_device, mesh=mesh, in_specs=in_specs, out_specs=out_specs, check_vma=False
    )
```
